32 devices in a mesh: ctx: 8 (over z, y), hg: 4 (over x, core).
Axes of the slice: x: 2, y: 2, z: 4, core: 2. Of those that a mesh axis runs over, the one named last changes fastest.
Arguments:
- query: bfloat16 [1024, 5120], P('ctx', 'hg'), may hold values from -6 to 6
- key: bfloat16 [1024, 5120], P('ctx', 'hg'), may hold values from -6 to 6
- value: bfloat16 [1024, 5120], P('ctx', 'hg'), may hold values from -6 to 6
- gate_logit: float32 [1024, 40], P('ctx', 'hg'), may hold values from -40 to 10
- exponent: int32 [40], P('hg'), may hold values from 0 to 6
- norm_gain: float32 [5120], P('hg'), may hold values from 0.5 to 1.5
- kv_weight: bfloat16 [5120, 2048], P('hg'), may hold values from -0.078125 to 0.078125
- cross_query: bfloat16 [1024, 5120], P('ctx', 'hg'), may hold values from -256 to 256
Outputs:
- retained: bfloat16 [1024, 5120], P('ctx', 'hg')
- attended: bfloat16 [1024, 5120], P('ctx', 'hg')
The draws below stay inside these ranges and needn't reach their ends.
All inputs are finite; a program needn't handle non-finite values.
Results may differ from the reference program's by a relative error of at most 0.013.
The reference program's roundings to bfloat16 on the way (of `weight`, `cache` and `prob`) count: a program that leaves them out, or rounds other values in their place, can miss the bound.
Values may be sent and summed in bfloat16 or wider, within the bound.
A program may use at most 128 MiB of HBM per device.

```python
import jax
import jax.numpy as jnp
from jax import lax

D = 5120
H = 40
HD = 128
KVH = 8
TOK_DEV = 128
TOKENS = 1024
N_CTX = 8


def draw_gate_logit(key, part):
    key = jax.random.fold_in(key, 11)
    base_key, spot_key, depth_key = jax.random.split(key, 3)
    logits = 4.0 + jnp.clip(jax.random.normal(base_key, (TOKENS, H), jnp.float32), -4.0, 4.0)
    places = jax.random.randint(spot_key, (12, H), 0, TOKENS)
    depth = -jax.random.uniform(depth_key, (12, H), jnp.float32, 20.0, 40.0)
    columns = jnp.broadcast_to(jnp.arange(H)[None, :], (12, H))
    return logits.at[places, columns].set(depth)


def draw_cross_query(key, part):
    key = jax.random.fold_in(key, 23)
    entry_key = jax.random.fold_in(key, 0)
    entries = jnp.clip(jax.random.normal(entry_key, (TOKENS, D), jnp.float32), -6.0, 6.0)
    return entries.astype(jnp.bfloat16)


def with_ends(result, own_key, least, top_value):
    spot = [jax.random.randint(jax.random.fold_in(own_key, axis), (), 0, length) for axis, length in enumerate(result.shape)]
    longest = result.shape.index(max(result.shape))
    neighbour = spot[:longest] + [(spot[longest] + 1) % result.shape[longest]] + spot[longest + 1:]
    return result.at[tuple(spot)].set(least).at[tuple(neighbour)].set(top_value)


def steps_of(key, extent, pieces, least, largest):
    def one(dim, shards_of):
        draws = jax.random.uniform(jax.random.fold_in(jax.random.fold_in(key, 6), dim), (shards_of,), jnp.float32, least / len(pieces), largest / len(pieces))
        return jnp.repeat(jnp.exp(draws), extent[dim] // shards_of).reshape((-1,) + (1,) * (len(extent) - dim - 1))

    factor_of = one(*pieces[0])
    for cut in pieces[1:]:
        factor_of = factor_of * one(*cut)
    return factor_of


def gaussian(key, extent, scale, reach, cuts=(), kind=jnp.bfloat16):
    level = steps_of(key, extent, cuts, -0.22, 0.18) if cuts else 1.0
    drawn = jax.random.normal(key, extent, jnp.float32) * scale * level
    return jnp.minimum(jnp.maximum(drawn, -reach), reach).astype(kind)


def setup_inputs(seed: int = 0) -> dict:
    seeds = jax.random.split(jax.random.key(seed), 9)
    return {
        "query": gaussian(seeds[0], (TOKENS, D), 1.0, 6.0, ((0, 8), (1, 4))),
        "key": gaussian(seeds[1], (TOKENS, D), 1.0, 6.0, ((0, 8), (1, 4))),
        "value": gaussian(seeds[2], (TOKENS, D), 1.0, 6.0, ((0, 8), (1, 4))),
        "gate_logit": draw_gate_logit(jax.random.fold_in(seeds[8], 71), 0),
        "exponent": with_ends(jax.random.randint(seeds[4], (H,), 0, 7), jax.random.fold_in(seeds[4], 1), 0, 6).astype(jnp.int32),
        "norm_gain": jnp.clip(1.0 + 0.1 * jax.random.normal(seeds[5], (D,), jnp.float32), 0.5, 1.5),
        "kv_weight": gaussian(seeds[6], (D, 2 * KVH * HD), D ** -0.5, 0.078125, ((0, 4),)),
        "cross_query": draw_cross_query(jax.random.fold_in(seeds[8], 71), 0),
    }


def reference(query, key, value, gate_logit, exponent, norm_gain, kv_weight, cross_query):
    scale = HD ** (-0.5)
    rate = jnp.exp2(-exponent.astype(jnp.float32))
    log_gate = jax.nn.log_sigmoid(gate_logit) * rate[None, :]
    qs = query.reshape(N_CTX, TOK_DEV, H, HD)
    ks = key.reshape(N_CTX, TOK_DEV, H, HD)
    vs = value.reshape(N_CTX, TOK_DEV, H, HD)
    gs = log_gate.reshape(N_CTX, TOK_DEV, H)
    lower = jnp.arange(TOK_DEV)[:, None] >= jnp.arange(TOK_DEV)[None, :]

    def block(state, items):
        qb, kb, vb, lb = items
        cumul = jnp.cumsum(lb, axis=0)
        total = cumul[-1]
        diff = jnp.transpose(cumul[:, None, :] - cumul[None, :, :], (2, 0, 1))
        decay = jnp.where(lower[None], jnp.exp(jnp.where(lower[None], diff, 0.0)), 0.0)
        scores = jnp.einsum('thd,shd->hts', qb.astype(jnp.float32), kb.astype(jnp.float32))
        weight = (scores * decay * scale).astype(jnp.bfloat16)
        local = jnp.einsum('hts,shd->thd', weight.astype(jnp.float32), vb.astype(jnp.float32))
        carried = jnp.einsum('thd,hde->the', qb.astype(jnp.float32), state, precision=lax.Precision.HIGHEST) * jnp.exp(cumul)[:, :, None]
        scaled_keys = kb.astype(jnp.float32) * (jnp.exp(total[None, :] - cumul) * scale)[:, :, None]
        fresh = jnp.einsum('thd,the->hde', scaled_keys, vb.astype(jnp.float32), precision=lax.Precision.HIGHEST)
        new_state = state * jnp.exp(total)[:, None, None] + fresh
        return (new_state, local + carried)
    start = jnp.zeros((H, HD, HD), jnp.float32)
    final, outs = lax.scan(block, start, (qs, ks, vs, gs))
    out = outs.reshape(TOKENS, H, HD)
    mean = lax.optimization_barrier(jnp.mean(out, axis=-1, keepdims=True))
    var = lax.optimization_barrier(jnp.mean((out - mean) ** 2, axis=-1, keepdims=True))
    normed = (out - mean) / jnp.sqrt(var + 1e-06) * norm_gain.reshape(H, HD)
    retained = normed.astype(jnp.bfloat16).reshape(TOKENS, D)
    cache = jnp.dot(retained, kv_weight, preferred_element_type=jnp.float32).astype(jnp.bfloat16)
    cache = cache.reshape(TOKENS, KVH, 2, HD)
    group = H // KVH
    cq = cross_query.reshape(TOKENS, H, HD)
    causal = jnp.arange(TOKENS)[:, None] >= jnp.arange(TOKENS)[None, :]

    def head(index):
        kv_index = index // group
        qh = lax.dynamic_index_in_dim(cq, index, 1, keepdims=False).astype(jnp.float32)
        pair = lax.dynamic_index_in_dim(cache, kv_index, 1, keepdims=False)
        keys_h = pair[:, 0, :].astype(jnp.float32)
        vals_h = pair[:, 1, :].astype(jnp.float32)
        score = jnp.dot(qh, keys_h.T) * scale
        score = jnp.where(causal, score, -1e+30)
        top = lax.optimization_barrier(jnp.max(score, axis=-1, keepdims=True))
        expo = jnp.where(causal, jnp.exp(score - top), 0.0)
        total = lax.optimization_barrier(jnp.sum(expo, axis=-1, keepdims=True))
        prob = expo.astype(jnp.bfloat16).astype(jnp.float32)
        return jnp.dot(prob, vals_h) / total
    heads_out = lax.map(head, jnp.arange(H, dtype=jnp.int32))
    attended = jnp.transpose(heads_out, (1, 0, 2)).reshape(TOKENS, D).astype(jnp.bfloat16)
    return (retained, attended)
```

```python
import functools

import jax
import jax.numpy as jnp
from jax import lax
from jax.experimental import pallas as pl
from jax.experimental.pallas import tpu as pltpu
from jax.sharding import PartitionSpec as P

HD = 128
F32 = jnp.float32
BF16 = jnp.bfloat16
MESH = pl.DeviceIdType.MESH


def dot(a, b, dims=((1,), (0,))):
    return lax.dot_general(a, b, (dims, ((), ())), preferred_element_type=F32)


def split(x):
    hi = x.astype(BF16)
    return hi, (x - hi.astype(F32)).astype(BF16)


def kernel(
    nz, nhg,
    q_ref, k_ref, v_ref, gate_ref, expo_ref, gain_ref, w_hbm, cq_ref,
    ret_ref, att_ref,
    w_vm, bcol, brow, dtot_ref, local_ref,
    own_f, send_f, recv_f, send_s, recv_s, send_e, recv_e,
    p1_send, p1_recv, p2_send, p2_recv, own_p,
    kv, cross, top_ref, den_ref, acc_ref,
    w_sem, fs, fr, ss, sr, es, er, p1s, p1r, p2s, p2r, zs, zr, ys, yr,
):
    tok, width = q_ref.shape
    heads = width // HD
    half = heads // 2
    share = w_vm.shape[1] // nhg
    kvh = share // (2 * HD)
    group = heads // kvh
    rows = group * tok
    scale = HD ** (-0.5)
    me = lax.axis_index("ctx")
    g = lax.axis_index("hg")
    z = me // 2
    y = me % 2
    partner = {"ctx": me + 1 - 2 * y, "hg": g}
    ahead = {"ctx": me + 2, "hg": g}
    behind = {"ctx": me - 2, "hg": g}
    g1 = g + 1 - 2 * (g % 2)
    g2 = (g + nhg // 2) % nhg
    g3 = (g1 + nhg // 2) % nhg
    near = {"ctx": me, "hg": g1}
    far = {"ctx": me, "hg": g2}
    first = z == 0
    last = z == nz - 1

    w_copy = pltpu.make_async_copy(w_hbm, w_vm, w_sem)
    w_copy.start()

    barrier = pltpu.get_barrier_semaphore()
    for who in (partner, near, far):
        pl.semaphore_signal(barrier, inc=1, device_id=who, device_id_type=MESH)

    @pl.when(jnp.logical_not(first))
    def _():
        pl.semaphore_signal(barrier, inc=1, device_id=behind, device_id_type=MESH)

    @pl.when(jnp.logical_not(last))
    def _():
        pl.semaphore_signal(barrier, inc=1, device_id=ahead, device_id_type=MESH)

    def send(src, dst, s_sem, r_sem, who):
        return pltpu.make_async_remote_copy(
            src_ref=src, dst_ref=dst, send_sem=s_sem, recv_sem=r_sem,
            device_id=who, device_id_type=MESH,
        )

    def cols(h, n=HD):
        return pl.ds(pl.multiple_of(h * n, n), n)

    x = gate_ref[...]
    rate = jnp.exp2(-expo_ref[...].astype(F32))
    log_gate = (jnp.minimum(x, 0.0) - jnp.log1p(jnp.exp(-jnp.abs(x)))) * rate
    log_gate = jnp.concatenate([log_gate, jnp.zeros((tok, HD - heads), F32)], axis=1)
    r_id = lax.broadcasted_iota(jnp.int32, (tok, tok), 0)
    c_id = lax.broadcasted_iota(jnp.int32, (tok, tok), 1)
    lower = r_id >= c_id
    cumul = lax.dot_general(
        lower.astype(F32), log_gate, (((1,), (0,)), ((), ())),
        precision=lax.Precision.HIGHEST, preferred_element_type=F32,
    )
    brow[...] = jnp.transpose(cumul)
    for h in range(heads):
        bcol[h] = jnp.broadcast_to(cumul[:, h : h + 1], (tok, HD))
        dtot_ref[h] = jnp.broadcast_to(jnp.exp(cumul[tok - 1 : tok, h : h + 1]), (8, HD))

    def fresh(h, out, j):
        total = bcol[h, tok - 1 : tok, :]
        keys = k_ref[:, cols(h)].astype(F32) * (jnp.exp(total - bcol[h]) * scale)
        hi, lo = split(keys)
        vals = v_ref[:, cols(h)]
        dims = ((0,), (0,))
        out[j, :HD, :] = dot(hi, vals, dims) + dot(lo, vals, dims)
        out[j, HD:, :] = dtot_ref[h]

    pl.semaphore_wait(barrier, 3 + jnp.where(first, 0, 1) + jnp.where(last, 0, 1))

    for j in range(half):
        fresh((1 - y) * half + j, send_f, j)
        send(send_f.at[j], recv_f.at[j], fs.at[j], fr.at[j], partner).start()
    for j in range(half):
        fresh(y * half + j, own_f, j)

    def pair(j):
        mine, his = own_f[j, :HD, :], recv_f[j, :HD, :]
        dm, dh = own_f[j, HD : HD + 1, :], recv_f[j, HD : HD + 1, :]
        even = y == 0
        f0, f1 = jnp.where(even, mine, his), jnp.where(even, his, mine)
        d0, d1 = jnp.where(even, dm, dh), jnp.where(even, dh, dm)
        return f0, f1, d0, d1

    def f_copy(j):
        return send(send_f.at[j], recv_f.at[j], fs.at[j], fr.at[j], partner)

    def s_copy(j):
        return send(send_s.at[j], recv_s.at[j], ss.at[j], sr.at[j], ahead)

    def e_copy(j):
        return send(send_e.at[j], recv_e.at[j], es.at[j], er.at[j], partner)

    @pl.when(first)
    def _():
        recv_s[...] = jnp.zeros_like(recv_s)

    for j in range(half):
        f_copy(j).wait_recv()
        f0, f1, d0, d1 = pair(j)
        send_s[j] = d1 * f0 + f1

        @pl.when(first)
        def _():
            s_copy(j).start()

    for h in range(heads):
        diff = jnp.minimum(bcol[h] - brow[h : h + 1, :], 0.0)
        decay = jnp.where(lower, jnp.exp(diff), 0.0)
        at = slice(h * HD, (h + 1) * HD)
        score = dot(q_ref[:, at], k_ref[:, at], ((1,), (1,)))
        weight = (score * decay * scale).astype(BF16)
        local_ref[h] = dot(weight, v_ref[:, at])

    for h in range(heads):
        c, i = h // group, h % group
        cross[c, i * tok : (i + 1) * tok, :] = cq_ref[:, h * HD : (h + 1) * HD]
    top_ref[...] = jnp.full_like(top_ref, -1e30)
    den_ref[...] = jnp.zeros_like(den_ref)
    acc_ref[...] = jnp.zeros_like(acc_ref)

    def finish(h, state):
        hi, lo = split(state)
        qh = q_ref[:, cols(h)]
        out = local_ref[h] + (dot(qh, hi) + dot(qh, lo)) * jnp.exp(bcol[h])
        mean = jnp.mean(out, axis=-1, keepdims=True)
        out = out - mean
        var = jnp.mean(out * out, axis=-1, keepdims=True)
        out = out / jnp.sqrt(var + 1e-06) * gain_ref[:, cols(h)]
        ret_ref[:, cols(h)] = out.astype(BF16)

    for j in range(half):
        @pl.when(jnp.logical_not(first))
        def _():
            s_copy(j).wait_recv()
            _, _, d0, d1 = pair(j)
            send_s[j] = (d0 * d1) * recv_s[j] + send_s[j]

            @pl.when(jnp.logical_not(last))
            def _():
                s_copy(j).start()

        f0, _, d0, _ = pair(j)
        s = recv_s[j]
        e1 = d0 * s + f0
        send_e[j] = jnp.where(y == 0, e1, s)
        e_copy(j).start()
        finish(y * half + j, jnp.where(y == 0, s, e1))
    for j in range(half):
        e_copy(j).wait_recv()
        finish((1 - y) * half + j, recv_e[j])

    w_copy.wait()
    wide = 2 * HD

    def p1_copy(c, b):
        return send(p1_send.at[c, b], p1_recv.at[c, b], p1s.at[c, b], p1r.at[c, b], near)

    def p2_copy(c):
        return send(p2_send.at[c], p2_recv.at[c], p2s.at[c], p2r.at[c], far)

    def part(dest, c):
        return dot(ret_ref[...], w_vm[:, cols(dest * kvh + c, wide)])

    for c in range(kvh):
        for b, dest in ((0, g3), (1, g1)):
            p1_send[c, b] = part(dest, c)
            p1_copy(c, b).start()
    for c in range(kvh):
        p2_send[c] = part(g2, c)
    for c in range(kvh):
        p1_copy(c, 0).wait_recv()
        p2_send[c] = p2_send[c] + p1_recv[c, 0]
        p2_copy(c).start()
    for c in range(kvh):
        own_p[c] = part(g, c)
        p1_copy(c, 1).wait_recv()
        own_p[c] = own_p[c] + p1_recv[c, 1]

    def spot(block, c):
        return kv.at[c, pl.ds(pl.multiple_of(block * tok, tok), tok), :]

    def z_copy(zz, c):
        at = spot(2 * zz + y, c)
        return send(at, at, zs.at[zz, c], zr.at[zz, c], ahead)

    def y_copy(zz, c):
        at = spot(2 * zz + y, c)
        return send(at, at, ys.at[zz, c], yr.at[zz, c], partner)

    def y_arrived(zz, c):
        at = spot(2 * zz + 1 - y, c)
        return send(at, at, ys.at[zz, c], yr.at[zz, c], partner)

    def attend(zz, c, masked):
        both = kv[c, pl.ds(pl.multiple_of(zz * 2 * tok, 2 * tok), 2 * tok), :]
        keys, vals = both[:, :HD], both[:, HD:]
        for i in range(group):
            at = slice(i * tok, (i + 1) * tok)
            score = dot(cross[c, at, :], keys, ((1,), (1,))) * scale
            if masked:
                q_pos = y * tok + lax.broadcasted_iota(jnp.int32, (tok, 2 * tok), 0)
                keep = lax.broadcasted_iota(jnp.int32, (tok, 2 * tok), 1) <= q_pos
                score = jnp.where(keep, score, -1e30)
            old = top_ref[c, at, :]
            new = jnp.maximum(old, jnp.max(score, axis=-1, keepdims=True))
            factor = jnp.exp(old - new)
            top_ref[c, at, :] = new
            new2 = jnp.concatenate([new, new], axis=1)
            expo = jnp.exp(score - new2)
            if masked:
                expo = jnp.where(keep, expo, 0.0)
            den_ref[c, at, :] = den_ref[c, at, :] * factor + (expo[:, :HD] + expo[:, HD:])
            acc_ref[c, at, :] = acc_ref[c, at, :] * factor + dot(expo.astype(BF16), vals)

    def earlier(zz, carry):
        for c in range(kvh):
            z_copy(zz, c).wait_recv()

            @pl.when(jnp.logical_not(last))
            def _():
                z_copy(zz, c).start()

            y_copy(zz, c).start()
        for c in range(kvh):
            y_arrived(zz, c).wait_recv()
            attend(zz, c, False)
        return carry

    lax.fori_loop(0, z, earlier, 0)

    for c in range(kvh):
        p2_copy(c).wait_recv()
        spot(me, c)[...] = (own_p[c] + p2_recv[c]).astype(BF16)

        @pl.when(y == 0)
        def _():
            y_copy(z, c).start()
            spot(me + 1, c)[...] = jnp.zeros((tok, wide), BF16)

        @pl.when(jnp.logical_not(last))
        def _():
            z_copy(z, c).start()

    for c in range(kvh):
        @pl.when(y == 1)
        def _():
            y_arrived(z, c).wait_recv()

        attend(z, c, True)
    for h in range(heads):
        c, i = h // group, h % group
        at = slice(i * tok, (i + 1) * tok)
        total = jnp.sum(den_ref[c, at, :], axis=-1, keepdims=True)
        att_ref[:, h * HD : (h + 1) * HD] = (acc_ref[c, at, :] / total).astype(BF16)

    for j in range(half):
        f_copy(j).wait_send()
        e_copy(j).wait_send()

        @pl.when(jnp.logical_not(last))
        def _():
            s_copy(j).wait_send()

    for c in range(kvh):
        p1_copy(c, 0).wait_send()
        p1_copy(c, 1).wait_send()
        p2_copy(c).wait_send()

        @pl.when(y == 0)
        def _():
            y_copy(z, c).wait_send()

        @pl.when(jnp.logical_not(last))
        def _():
            z_copy(z, c).wait_send()

    def drain(zz, carry):
        for c in range(kvh):
            y_copy(zz, c).wait_send()

            @pl.when(jnp.logical_not(last))
            def _():
                z_copy(zz, c).wait_send()

        return carry

    lax.fori_loop(0, z, drain, 0)


def body(nctx, nhg, query, key, value, gate_logit, exponent, norm_gain, kv_weight, cross_query):
    tok, width = query.shape
    heads = width // HD
    half = heads // 2
    nz = nctx // 2
    share = kv_weight.shape[1] // nhg
    kvh = share // (2 * HD)
    rows = heads // kvh * tok
    vmem = pl.BlockSpec(memory_space=pltpu.VMEM)
    dma = pltpu.SemaphoreType.DMA
    return pl.pallas_call(
        functools.partial(kernel, nz, nhg),
        out_shape=(
            jax.ShapeDtypeStruct((tok, width), BF16),
            jax.ShapeDtypeStruct((tok, width), BF16),
        ),
        in_specs=[vmem] * 6 + [pl.BlockSpec(memory_space=pl.ANY), vmem],
        out_specs=(vmem, vmem),
        scratch_shapes=[
            pltpu.VMEM(kv_weight.shape, BF16),
            pltpu.VMEM((heads, tok, HD), F32),
            pltpu.VMEM((HD, tok), F32),
            pltpu.VMEM((heads, 8, HD), F32),
            pltpu.VMEM((heads, tok, HD), F32),
            pltpu.VMEM((half, HD + 8, HD), F32),
            pltpu.VMEM((half, HD + 8, HD), F32),
            pltpu.VMEM((half, HD + 8, HD), F32),
            pltpu.VMEM((half, HD, HD), F32),
            pltpu.VMEM((half, HD, HD), F32),
            pltpu.VMEM((half, HD, HD), F32),
            pltpu.VMEM((half, HD, HD), F32),
            pltpu.VMEM((kvh, 2, tok, 2 * HD), F32),
            pltpu.VMEM((kvh, 2, tok, 2 * HD), F32),
            pltpu.VMEM((kvh, tok, 2 * HD), F32),
            pltpu.VMEM((kvh, tok, 2 * HD), F32),
            pltpu.VMEM((kvh, tok, 2 * HD), F32),
            pltpu.VMEM((kvh, nctx * tok, 2 * HD), BF16),
            pltpu.VMEM((kvh, rows, HD), BF16),
            pltpu.VMEM((kvh, rows, HD), F32),
            pltpu.VMEM((kvh, rows, HD), F32),
            pltpu.VMEM((kvh, rows, HD), F32),
            dma,
            dma((half,)), dma((half,)), dma((half,)), dma((half,)), dma((half,)), dma((half,)),
            dma((kvh, 2)), dma((kvh, 2)), dma((kvh,)), dma((kvh,)),
            dma((nz, kvh)), dma((nz, kvh)), dma((nz, kvh)), dma((nz, kvh)),
        ],
        compiler_params=pltpu.CompilerParams(
            collective_id=0, has_side_effects=True, vmem_limit_bytes=48 * 1024 * 1024
        ),
    )(
        query, key, value, gate_logit, exponent.reshape(1, heads),
        norm_gain.reshape(1, width), kv_weight, cross_query,
    )


def solution(mesh):
    spec = P("ctx", "hg")
    in_specs = (spec, spec, spec, spec, P("hg"), P("hg"), P("hg", None), spec)
    return jax.shard_map(
        functools.partial(body, mesh.shape["ctx"], mesh.shape["hg"]),
        mesh=mesh, in_specs=in_specs, out_specs=(spec, spec), check_vma=False,
    )
```

```python
import functools

import jax
import jax.numpy as jnp
from jax import lax
from jax.experimental import pallas as pl
from jax.experimental.pallas import tpu as pltpu
from jax.sharding import PartitionSpec as P

HD = 128
F32 = jnp.float32
BF16 = jnp.bfloat16
MESH = pl.DeviceIdType.MESH


def dot(a, b, dims=((1,), (0,))):
    return lax.dot_general(a, b, (dims, ((), ())), preferred_element_type=F32)


def split(x):
    hi = x.astype(BF16)
    return hi, (x - hi.astype(F32)).astype(BF16)


def kernel(
    nz, nhg,
    q_hbm, k_hbm, v_hbm, gate_hbm, expo_hbm, gain_hbm, w_hbm, cq_hbm,
    ret_ref, att_ref,
    q_ref, k_ref, v_ref, cq_ref, gate_ref, expo_ref, gain_ref, gate_pad,
    w_vm, bcol, brow, dtot_ref, local_ref,
    own_f, send_f, recv_f, send_s, recv_s, send_e, recv_e,
    p1_send, p1_recv, p2_send, p2_recv, own_p,
    kv, cross, top_ref, den_ref, acc_ref,
    in_sem, fs, fr, ss, sr, es, er, p1s, p1r, p2s, p2r, zs, zr, ys, yr,
):
    tok, width = q_ref.shape
    heads = width // HD
    half = heads // 2
    share = w_vm.shape[1] // nhg
    kvh = share // (2 * HD)
    group = heads // kvh
    rows = group * tok
    scale = HD ** (-0.5)
    me = lax.axis_index("ctx")
    g = lax.axis_index("hg")
    z = me // 2
    y = me % 2
    partner = {"ctx": me + 1 - 2 * y, "hg": g}
    ahead = {"ctx": me + 2, "hg": g}
    behind = {"ctx": me - 2, "hg": g}
    g1 = g + 1 - 2 * (g % 2)
    g2 = (g + nhg // 2) % nhg
    g3 = (g1 + nhg // 2) % nhg
    near = {"ctx": me, "hg": g1}
    far = {"ctx": me, "hg": g2}
    first = z == 0
    last = z == nz - 1

    copies = [
        pltpu.make_async_copy(src, dst, in_sem.at[i])
        for i, (src, dst) in enumerate((
            (gate_hbm, gate_ref), (expo_hbm, expo_ref), (k_hbm, k_ref), (v_hbm, v_ref),
            (q_hbm, q_ref), (cq_hbm, cq_ref), (gain_hbm, gain_ref), (w_hbm, w_vm),
        ))
    ]
    for copy in copies:
        copy.start()
    gate_copy, expo_copy, k_copy, v_copy, q_copy, cq_copy, gain_copy, w_copy = copies

    barrier = pltpu.get_barrier_semaphore()
    for who in (partner, near, far):
        pl.semaphore_signal(barrier, inc=1, device_id=who, device_id_type=MESH)

    @pl.when(jnp.logical_not(first))
    def _():
        pl.semaphore_signal(barrier, inc=1, device_id=behind, device_id_type=MESH)

    @pl.when(jnp.logical_not(last))
    def _():
        pl.semaphore_signal(barrier, inc=1, device_id=ahead, device_id_type=MESH)

    def send(src, dst, s_sem, r_sem, who):
        return pltpu.make_async_remote_copy(
            src_ref=src, dst_ref=dst, send_sem=s_sem, recv_sem=r_sem,
            device_id=who, device_id_type=MESH,
        )

    def cols(h, n=HD):
        return pl.ds(pl.multiple_of(h * n, n), n)

    gate_copy.wait()
    expo_copy.wait()
    x = gate_ref[...]
    rate = jnp.exp2(-expo_ref[...].astype(F32))
    rate = jnp.concatenate([rate, jnp.zeros((1, HD - heads), F32)], axis=1)
    gate_pad[...] = jnp.zeros_like(gate_pad)
    gate_pad[:heads, :] = jnp.minimum(x, 0.0) - jnp.log1p(jnp.exp(-jnp.abs(x)))
    log_gate = jnp.transpose(gate_pad[...]) * rate
    r_id = lax.broadcasted_iota(jnp.int32, (tok, tok), 0)
    c_id = lax.broadcasted_iota(jnp.int32, (tok, tok), 1)
    lower = r_id >= c_id
    cumul = lax.dot_general(
        lower.astype(F32), log_gate, (((1,), (0,)), ((), ())),
        precision=lax.Precision.HIGHEST, preferred_element_type=F32,
    )
    brow[...] = jnp.transpose(cumul)
    for h in range(heads):
        bcol[h] = jnp.broadcast_to(cumul[:, h : h + 1], (tok, HD))
        dtot_ref[h] = jnp.broadcast_to(jnp.exp(cumul[tok - 1 : tok, h : h + 1]), (8, HD))

    def fresh(h, out, j):
        total = bcol[h, tok - 1 : tok, :]
        keys = k_ref[:, cols(h)].astype(F32) * (jnp.exp(total - bcol[h]) * scale)
        hi, lo = split(keys)
        vals = v_ref[:, cols(h)]
        dims = ((0,), (0,))
        out[j, :HD, :] = dot(hi, vals, dims) + dot(lo, vals, dims)
        out[j, HD:, :] = dtot_ref[h]

    pl.semaphore_wait(barrier, 3 + jnp.where(first, 0, 1) + jnp.where(last, 0, 1))

    k_copy.wait()
    v_copy.wait()
    for j in range(half):
        fresh((1 - y) * half + j, send_f, j)
        send(send_f.at[j], recv_f.at[j], fs.at[j], fr.at[j], partner).start()
    for j in range(half):
        fresh(y * half + j, own_f, j)

    def pair(j):
        mine, his = own_f[j, :HD, :], recv_f[j, :HD, :]
        dm, dh = own_f[j, HD : HD + 1, :], recv_f[j, HD : HD + 1, :]
        even = y == 0
        f0, f1 = jnp.where(even, mine, his), jnp.where(even, his, mine)
        d0, d1 = jnp.where(even, dm, dh), jnp.where(even, dh, dm)
        return f0, f1, d0, d1

    def f_copy(j):
        return send(send_f.at[j], recv_f.at[j], fs.at[j], fr.at[j], partner)

    def s_copy(j):
        return send(send_s.at[j], recv_s.at[j], ss.at[j], sr.at[j], ahead)

    def e_copy(j):
        return send(send_e.at[j], recv_e.at[j], es.at[j], er.at[j], partner)

    @pl.when(first)
    def _():
        recv_s[...] = jnp.zeros_like(recv_s)

    for j in range(half):
        f_copy(j).wait_recv()
        f0, f1, d0, d1 = pair(j)
        send_s[j] = d1 * f0 + f1

        @pl.when(first)
        def _():
            s_copy(j).start()

    q_copy.wait()
    for h in range(heads):
        diff = jnp.minimum(bcol[h] - brow[h : h + 1, :], 0.0)
        decay = jnp.where(lower, jnp.exp(diff), 0.0)
        at = slice(h * HD, (h + 1) * HD)
        score = dot(q_ref[:, at], k_ref[:, at], ((1,), (1,)))
        weight = (score * decay * scale).astype(BF16)
        local_ref[h] = dot(weight, v_ref[:, at])

    cq_copy.wait()
    gain_copy.wait()
    for h in range(heads):
        c, i = h // group, h % group
        cross[c, i * tok : (i + 1) * tok, :] = cq_ref[:, h * HD : (h + 1) * HD]
    top_ref[...] = jnp.full_like(top_ref, -1e30)
    den_ref[...] = jnp.zeros_like(den_ref)
    acc_ref[...] = jnp.zeros_like(acc_ref)

    def finish(h, state):
        hi, lo = split(state)
        qh = q_ref[:, cols(h)]
        out = local_ref[h] + (dot(qh, hi) + dot(qh, lo)) * jnp.exp(bcol[h])
        mean = jnp.mean(out, axis=-1, keepdims=True)
        out = out - mean
        var = jnp.mean(out * out, axis=-1, keepdims=True)
        out = out / jnp.sqrt(var + 1e-06) * gain_ref[pl.ds(h, 1), :]
        ret_ref[:, cols(h)] = out.astype(BF16)

    lag = min(2, half)
    for j in range(half):
        @pl.when(jnp.logical_not(first))
        def _():
            s_copy(j).wait_recv()
            _, _, d0, d1 = pair(j)
            send_s[j] = (d0 * d1) * recv_s[j] + send_s[j]

            @pl.when(jnp.logical_not(last))
            def _():
                s_copy(j).start()

        f0, _, d0, _ = pair(j)
        s = recv_s[j]
        e1 = d0 * s + f0
        send_e[j] = jnp.where(y == 0, e1, s)
        e_copy(j).start()
        finish(y * half + j, jnp.where(y == 0, s, e1))
        if j >= lag:
            e_copy(j - lag).wait_recv()
            finish((1 - y) * half + j - lag, recv_e[j - lag])
    for j in range(half - lag, half):
        e_copy(j).wait_recv()
    for j in range(half - lag, half):
        finish((1 - y) * half + j, recv_e[j])

    w_copy.wait()
    wide = 2 * HD

    def p1_copy(c, b):
        return send(p1_send.at[c, b], p1_recv.at[c, b], p1s.at[c, b], p1r.at[c, b], near)

    def p2_copy(c):
        return send(p2_send.at[c], p2_recv.at[c], p2s.at[c], p2r.at[c], far)

    def part(dest, c):
        return dot(ret_ref[...], w_vm[:, cols(dest * kvh + c, wide)])

    for c in range(kvh):
        for b, dest in ((0, g3), (1, g1)):
            p1_send[c, b] = part(dest, c)
            p1_copy(c, b).start()
    for c in range(kvh):
        p2_send[c] = part(g2, c)
    for c in range(kvh):
        p1_copy(c, 0).wait_recv()
        p2_send[c] = p2_send[c] + p1_recv[c, 0]
        p2_copy(c).start()
    for c in range(kvh):
        own_p[c] = part(g, c)
        p1_copy(c, 1).wait_recv()
        own_p[c] = own_p[c] + p1_recv[c, 1]

    def spot(block, c):
        return kv.at[c, pl.ds(pl.multiple_of(block * tok, tok), tok), :]

    def z_copy(zz, c):
        at = spot(2 * zz + y, c)
        return send(at, at, zs.at[zz, c], zr.at[zz, c], ahead)

    def y_copy(zz, c):
        at = spot(2 * zz + y, c)
        return send(at, at, ys.at[zz, c], yr.at[zz, c], partner)

    def y_arrived(zz, c):
        at = spot(2 * zz + 1 - y, c)
        return send(at, at, ys.at[zz, c], yr.at[zz, c], partner)

    def attend(zz, c, masked):
        both = kv[c, pl.ds(pl.multiple_of(zz * 2 * tok, 2 * tok), 2 * tok), :]
        keys, vals = both[:, :HD], both[:, HD:]
        score = dot(cross[c], keys, ((1,), (1,))) * scale
        if masked:
            q_pos = y * tok + lax.broadcasted_iota(jnp.int32, (tok, 2 * tok), 0)
            keep = lax.broadcasted_iota(jnp.int32, (tok, 2 * tok), 1) <= q_pos
            keep = jnp.concatenate([jnp.where(keep, 1.0, 0.0)] * group, axis=0) > 0.5
            score = jnp.where(keep, score, -1e30)
        old = top_ref[c]
        new = jnp.maximum(old, jnp.max(score, axis=-1, keepdims=True))
        factor = jnp.exp(old - new)
        top_ref[c] = new
        expo = jnp.exp(score - jnp.concatenate([new, new], axis=1))
        if masked:
            expo = jnp.where(keep, expo, 0.0)
        den_ref[c] = den_ref[c] * factor + (expo[:, :HD] + expo[:, HD:])
        acc_ref[c] = acc_ref[c] * factor + dot(expo.astype(BF16), vals)

    def earlier(zz, carry):
        for c in range(kvh):
            z_copy(zz, c).wait_recv()

            @pl.when(jnp.logical_not(last))
            def _():
                z_copy(zz, c).start()

            y_copy(zz, c).start()
        for c in range(kvh):
            y_arrived(zz, c).wait_recv()
            attend(zz, c, False)
        return carry

    lax.fori_loop(0, z - 1, earlier, 0)

    for c in range(kvh):
        p2_copy(c).wait_recv()
        spot(me, c)[...] = (own_p[c] + p2_recv[c]).astype(BF16)

        @pl.when(y == 0)
        def _():
            y_copy(z, c).start()
            spot(me + 1, c)[...] = jnp.zeros((tok, wide), BF16)

        @pl.when(jnp.logical_not(last))
        def _():
            z_copy(z, c).start()

    @pl.when(jnp.logical_not(first))
    def _():
        earlier(z - 1, 0)

    for c in range(kvh):
        @pl.when(y == 1)
        def _():
            y_arrived(z, c).wait_recv()

        attend(z, c, True)
    for h in range(heads):
        c, i = h // group, h % group
        at = slice(i * tok, (i + 1) * tok)
        total = jnp.sum(den_ref[c, at, :], axis=-1, keepdims=True)
        att_ref[:, h * HD : (h + 1) * HD] = (acc_ref[c, at, :] / total).astype(BF16)

    for j in range(half):
        f_copy(j).wait_send()
        e_copy(j).wait_send()

        @pl.when(jnp.logical_not(last))
        def _():
            s_copy(j).wait_send()

    for c in range(kvh):
        p1_copy(c, 0).wait_send()
        p1_copy(c, 1).wait_send()
        p2_copy(c).wait_send()

        @pl.when(y == 0)
        def _():
            y_copy(z, c).wait_send()

        @pl.when(jnp.logical_not(last))
        def _():
            z_copy(z, c).wait_send()

    def drain(zz, carry):
        for c in range(kvh):
            y_copy(zz, c).wait_send()

            @pl.when(jnp.logical_not(last))
            def _():
                z_copy(zz, c).wait_send()

        return carry

    lax.fori_loop(0, z, drain, 0)


def body(nctx, nhg, query, key, value, gate_logit, exponent, norm_gain, kv_weight, cross_query):
    tok, width = query.shape
    heads = width // HD
    half = heads // 2
    nz = nctx // 2
    share = kv_weight.shape[1] // nhg
    kvh = share // (2 * HD)
    rows = heads // kvh * tok
    vmem = pl.BlockSpec(memory_space=pltpu.VMEM)
    hbm = pl.BlockSpec(memory_space=pltpu.HBM)
    dma = pltpu.SemaphoreType.DMA
    return pl.pallas_call(
        functools.partial(kernel, nz, nhg),
        out_shape=(
            jax.ShapeDtypeStruct((tok, width), BF16),
            jax.ShapeDtypeStruct((tok, width), BF16),
        ),
        in_specs=[hbm] * 8,
        out_specs=(vmem, vmem),
        scratch_shapes=[
            pltpu.VMEM((tok, width), BF16),
            pltpu.VMEM((tok, width), BF16),
            pltpu.VMEM((tok, width), BF16),
            pltpu.VMEM((tok, width), BF16),
            pltpu.VMEM((heads, tok), F32),
            pltpu.VMEM((1, heads), jnp.int32),
            pltpu.VMEM((heads, HD), F32),
            pltpu.VMEM((HD, tok), F32),
            pltpu.VMEM(kv_weight.shape, BF16),
            pltpu.VMEM((heads, tok, HD), F32),
            pltpu.VMEM((HD, tok), F32),
            pltpu.VMEM((heads, 8, HD), F32),
            pltpu.VMEM((heads, tok, HD), F32),
            pltpu.VMEM((half, HD + 8, HD), F32),
            pltpu.VMEM((half, HD + 8, HD), F32),
            pltpu.VMEM((half, HD + 8, HD), F32),
            pltpu.VMEM((half, HD, HD), F32),
            pltpu.VMEM((half, HD, HD), F32),
            pltpu.VMEM((half, HD, HD), F32),
            pltpu.VMEM((half, HD, HD), F32),
            pltpu.VMEM((kvh, 2, tok, 2 * HD), F32),
            pltpu.VMEM((kvh, 2, tok, 2 * HD), F32),
            pltpu.VMEM((kvh, tok, 2 * HD), F32),
            pltpu.VMEM((kvh, tok, 2 * HD), F32),
            pltpu.VMEM((kvh, tok, 2 * HD), F32),
            pltpu.VMEM((kvh, nctx * tok, 2 * HD), BF16),
            pltpu.VMEM((kvh, rows, HD), BF16),
            pltpu.VMEM((kvh, rows, HD), F32),
            pltpu.VMEM((kvh, rows, HD), F32),
            pltpu.VMEM((kvh, rows, HD), F32),
            dma((8,)),
            dma((half,)), dma((half,)), dma((half,)), dma((half,)), dma((half,)), dma((half,)),
            dma((kvh, 2)), dma((kvh, 2)), dma((kvh,)), dma((kvh,)),
            dma((nz, kvh)), dma((nz, kvh)), dma((nz, kvh)), dma((nz, kvh)),
        ],
        compiler_params=pltpu.CompilerParams(
            collective_id=0, has_side_effects=True, vmem_limit_bytes=56 * 1024 * 1024
        ),
    )(
        query, key, value, gate_logit.T, exponent.reshape(1, heads),
        norm_gain.reshape(heads, HD), kv_weight, cross_query,
    )


def solution(mesh):
    spec = P("ctx", "hg")
    in_specs = (spec, spec, spec, spec, P("hg"), P("hg"), P("hg", None), spec)
    return jax.shard_map(
        functools.partial(body, mesh.shape["ctx"], mesh.shape["hg"]),
        mesh=mesh, in_specs=in_specs, out_specs=(spec, spec), check_vma=False,
    )
```

```python
import functools

import jax
import jax.numpy as jnp
from jax import lax
from jax.experimental import pallas as pl
from jax.experimental.pallas import tpu as pltpu
from jax.sharding import PartitionSpec as P

HD = 128
F32 = jnp.float32
BF16 = jnp.bfloat16
MESH = pl.DeviceIdType.MESH


def dot(a, b, dims=((1,), (0,))):
    return lax.dot_general(a, b, (dims, ((), ())), preferred_element_type=F32)


def carry(q, state):
    hi, lo = split(state)
    return dot(q, hi) + dot(q, lo)


def split(x):
    hi = x.astype(BF16)
    return hi, (x - hi.astype(F32)).astype(BF16)


def kernel(
    nz, nhg,
    q_hbm, k_hbm, v_hbm, gate_hbm, expo_hbm, gain_hbm, w_hbm, cq_hbm,
    ret_hbm, att_hbm,
    ret_ref, att_ref, q_ref, k_ref, v_ref, cq_ref, gate_ref, expo_ref, gain_ref, gate_pad,
    w_vm, bcol, brow, dtot_ref, local_ref,
    own_f, send_f, recv_f, recv_d, send_s, recv_s, send_e, recv_e,
    p1_send, p1_recv, p2_send, p2_recv, own_p,
    kv, cross, top_ref, den_ref, acc_ref,
    in_sem, out_sem, d_sem, fs, fr, ss, sr, es, er, p1s, p1r, p2s, p2r, zs, zr, ys, yr,
):
    tok, width = q_ref.shape
    heads = width // HD
    half = heads // 2
    share = w_vm.shape[1] // nhg
    kvh = share // (2 * HD)
    group = heads // kvh
    rows = group * tok
    scale = HD ** (-0.5)
    me = lax.axis_index("ctx")
    g = lax.axis_index("hg")
    z = me // 2
    y = me % 2
    partner = {"ctx": me + 1 - 2 * y, "hg": g}
    ahead = {"ctx": me + 2, "hg": g}
    behind = {"ctx": me - 2, "hg": g}
    g1 = g + 1 - 2 * (g % 2)
    g2 = (g + nhg // 2) % nhg
    g3 = (g1 + nhg // 2) % nhg
    near = {"ctx": me, "hg": g1}
    far = {"ctx": me, "hg": g2}
    first = z == 0
    last = z == nz - 1

    copies = [
        pltpu.make_async_copy(src, dst, in_sem.at[i])
        for i, (src, dst) in enumerate((
            (gate_hbm, gate_ref), (expo_hbm, expo_ref), (k_hbm, k_ref), (v_hbm, v_ref),
            (q_hbm, q_ref), (cq_hbm, cq_ref), (gain_hbm, gain_ref), (w_hbm, w_vm),
        ))
    ]
    for copy in copies:
        copy.start()
    gate_copy, expo_copy, k_copy, v_copy, q_copy, cq_copy, gain_copy, w_copy = copies

    barrier = pltpu.get_barrier_semaphore()
    for who in (partner, near, far):
        pl.semaphore_signal(barrier, inc=1, device_id=who, device_id_type=MESH)

    @pl.when(jnp.logical_not(first))
    def _():
        pl.semaphore_signal(barrier, inc=1, device_id=behind, device_id_type=MESH)

    @pl.when(jnp.logical_not(last))
    def _():
        pl.semaphore_signal(barrier, inc=1, device_id=ahead, device_id_type=MESH)

    def send(src, dst, s_sem, r_sem, who):
        return pltpu.make_async_remote_copy(
            src_ref=src, dst_ref=dst, send_sem=s_sem, recv_sem=r_sem,
            device_id=who, device_id_type=MESH,
        )

    def cols(h, n=HD):
        return pl.ds(pl.multiple_of(h * n, n), n)

    gate_copy.wait()
    expo_copy.wait()
    x = gate_ref[...]
    rate = jnp.exp2(-expo_ref[...].astype(F32))
    rate = jnp.concatenate([rate, jnp.zeros((1, HD - heads), F32)], axis=1)
    gate_pad[...] = jnp.zeros_like(gate_pad)
    gate_pad[:heads, :] = jnp.minimum(x, 0.0) - jnp.log1p(jnp.exp(-jnp.abs(x)))
    log_gate = jnp.transpose(gate_pad[...]) * rate
    r_id = lax.broadcasted_iota(jnp.int32, (tok, tok), 0)
    c_id = lax.broadcasted_iota(jnp.int32, (tok, tok), 1)
    lower = r_id >= c_id
    cumul = lax.dot_general(
        lower.astype(F32), log_gate, (((1,), (0,)), ((), ())),
        precision=lax.Precision.HIGHEST, preferred_element_type=F32,
    )
    brow[...] = jnp.transpose(cumul)
    for h in range(heads):
        bcol[h] = jnp.broadcast_to(cumul[:, h : h + 1], (tok, HD))

    pad = dtot_ref.shape[0]
    dtot_ref[...] = jnp.exp(jnp.broadcast_to(brow[:pad, tok - 1 : tok], (pad, HD)))

    def fresh(h):
        total = bcol[h, tok - 1 : tok, :]
        keys = k_ref[:, cols(h)].astype(F32) * (jnp.exp(total - bcol[h]) * scale)
        hi, lo = split(keys)
        vals = v_ref[:, cols(h)]
        dims = ((0,), (0,))
        return dot(hi, vals, dims) + dot(lo, vals, dims)

    pl.semaphore_wait(barrier, 3 + jnp.where(first, 0, 1) + jnp.where(last, 0, 1))

    k_copy.wait()
    v_copy.wait()
    d_copy = send(dtot_ref, recv_d, d_sem.at[0], d_sem.at[1], partner)
    d_copy.start()
    for j in range(half):
        send_f[j] = fresh((1 - y) * half + j)
        send(send_f.at[j], recv_f.at[j], fs.at[j], fr.at[j], partner).start()
    for j in range(half):
        own_f[j] = fresh(y * half + j)

    def pair(j):
        mine, his = own_f[j], recv_f[j]
        row = pl.ds(y * half + j, 1)
        dm, dh = dtot_ref[row, :], recv_d[row, :]
        even = y == 0
        f0, f1 = jnp.where(even, mine, his), jnp.where(even, his, mine)
        d0, d1 = jnp.where(even, dm, dh), jnp.where(even, dh, dm)
        return f0, f1, d0, d1

    def f_copy(j):
        return send(send_f.at[j], recv_f.at[j], fs.at[j], fr.at[j], partner)

    def s_copy(j):
        return send(send_s.at[j], recv_s.at[j], ss.at[j], sr.at[j], ahead)

    def e_copy(j):
        return send(send_e.at[j], recv_e.at[j], es.at[j], er.at[j], partner)

    @pl.when(first)
    def _():
        recv_s[...] = jnp.zeros_like(recv_s)

    d_copy.wait()
    for j in range(half):
        f_copy(j).wait_recv()
        f0, f1, d0, d1 = pair(j)
        send_s[j] = d1 * f0 + f1

        @pl.when(first)
        def _():
            s_copy(j).start()

    q_copy.wait()
    for h in range(heads):
        diff = jnp.minimum(bcol[h] - brow[h : h + 1, :], 0.0)
        decay = jnp.where(lower, jnp.exp(diff), 0.0)
        at = slice(h * HD, (h + 1) * HD)
        score = dot(q_ref[:, at], k_ref[:, at], ((1,), (1,)))
        weight = (score * decay * scale).astype(BF16)
        local_ref[h] = dot(weight, v_ref[:, at])

    cq_copy.wait()
    gain_copy.wait()
    for h in range(heads):
        c, i = h // group, h % group
        cross[c, i * tok : (i + 1) * tok, :] = cq_ref[:, h * HD : (h + 1) * HD]
    top_ref[...] = jnp.full_like(top_ref, -1e30)
    den_ref[...] = jnp.zeros_like(den_ref)
    acc_ref[...] = jnp.zeros_like(acc_ref)

    def finish(h, state):
        out = local_ref[h] + carry(q_ref[:, cols(h)], state) * jnp.exp(bcol[h])
        mean = jnp.mean(out, axis=-1, keepdims=True)
        out = out - mean
        var = jnp.mean(out * out, axis=-1, keepdims=True)
        out = out / jnp.sqrt(var + 1e-06) * gain_ref[pl.ds(h, 1), :]
        ret_ref[:, cols(h)] = out.astype(BF16)

    lag = min(2, half)
    for j in range(half):
        @pl.when(jnp.logical_not(first))
        def _():
            s_copy(j).wait_recv()
            _, _, d0, d1 = pair(j)
            send_s[j] = (d0 * d1) * recv_s[j] + send_s[j]

            @pl.when(jnp.logical_not(last))
            def _():
                s_copy(j).start()

        f0, _, d0, _ = pair(j)
        s = recv_s[j]
        e1 = d0 * s + f0
        send_e[j] = jnp.where(y == 0, e1, s)
        e_copy(j).start()
        finish(y * half + j, jnp.where(y == 0, s, e1))
        if j >= lag:
            e_copy(j - lag).wait_recv()
            finish((1 - y) * half + j - lag, recv_e[j - lag])
    for j in range(half - lag, half):
        e_copy(j).wait_recv()
    for j in range(half - lag, half):
        finish((1 - y) * half + j, recv_e[j])

    ret_copy = pltpu.make_async_copy(ret_ref, ret_hbm, out_sem.at[kvh])
    ret_copy.start()
    w_copy.wait()
    wide = 2 * HD

    def p1_copy(c, b):
        return send(p1_send.at[c, b], p1_recv.at[c, b], p1s.at[c, b], p1r.at[c, b], near)

    def p2_copy(c):
        return send(p2_send.at[c], p2_recv.at[c], p2s.at[c], p2r.at[c], far)

    def part(dest, c):
        return dot(ret_ref[...], w_vm[:, cols(dest * kvh + c, wide)])

    for c in range(kvh):
        p1_send[c, 0] = part(g3, c)
        p1_copy(c, 0).start()
    for c in range(kvh):
        p2_send[c] = part(g2, c)
        p1_copy(c, 0).wait_recv()
        p2_send[c] = p2_send[c] + p1_recv[c, 0]
        p2_copy(c).start()
    for c in range(kvh):
        p1_send[c, 1] = part(g1, c)
        p1_copy(c, 1).start()
    for c in range(kvh):
        own_p[c] = part(g, c)
    for c in range(kvh):
        p1_copy(c, 1).wait_recv()
        own_p[c] = own_p[c] + p1_recv[c, 1]

    def spot(block, c):
        return kv.at[c, pl.ds(pl.multiple_of(block * tok, tok), tok), :]

    def z_copy(zz, c):
        at = spot(2 * zz + y, c)
        return send(at, at, zs.at[zz, c], zr.at[zz, c], ahead)

    def y_copy(zz, c):
        at = spot(2 * zz + y, c)
        return send(at, at, ys.at[zz, c], yr.at[zz, c], partner)

    def y_arrived(zz, c):
        at = spot(2 * zz + 1 - y, c)
        return send(at, at, ys.at[zz, c], yr.at[zz, c], partner)

    def attend(zz, c, masked):
        both = kv[c, pl.ds(pl.multiple_of(zz * 2 * tok, 2 * tok), 2 * tok), :]
        keys, vals = both[:, :HD], both[:, HD:]
        score = dot(cross[c], keys, ((1,), (1,))) * scale
        if masked:
            q_pos = y * tok + lax.broadcasted_iota(jnp.int32, (tok, 2 * tok), 0)
            keep = lax.broadcasted_iota(jnp.int32, (tok, 2 * tok), 1) <= q_pos
            keep = jnp.concatenate([jnp.where(keep, 1.0, 0.0)] * group, axis=0) > 0.5
            score = jnp.where(keep, score, -1e30)
        old = top_ref[c]
        new = jnp.maximum(old, jnp.max(score, axis=-1, keepdims=True))
        factor = jnp.exp(old - new)
        top_ref[c] = new
        expo = jnp.exp(score - jnp.concatenate([new, new], axis=1))
        if masked:
            expo = jnp.where(keep, expo, 0.0)
        den_ref[c] = den_ref[c] * factor + (expo[:, :HD] + expo[:, HD:])
        acc_ref[c] = acc_ref[c] * factor + dot(expo.astype(BF16), vals)

    for c in range(kvh):
        p2_copy(c).wait_recv()
        spot(me, c)[...] = (own_p[c] + p2_recv[c]).astype(BF16)

        @pl.when(y == 0)
        def _():
            y_copy(z, c).start()
            spot(me + 1, c)[...] = jnp.zeros((tok, wide), BF16)

        @pl.when(jnp.logical_not(last))
        def _():
            z_copy(z, c).start()

    def relay(zz):
        for c in range(kvh):
            z_copy(zz, c).wait_recv()

            @pl.when(jnp.logical_not(last))
            def _():
                z_copy(zz, c).start()

            y_copy(zz, c).start()

    def use(zz):
        for c in range(kvh):
            y_arrived(zz, c).wait_recv()
            attend(zz, c, False)

    @pl.when(jnp.logical_not(first))
    def _():
        relay(z - 1)

    for c in range(kvh):
        @pl.when(y == 1)
        def _():
            y_arrived(z, c).wait_recv()

        attend(z, c, True)

    def step(n, carry):
        relay(z - n)
        use(z - n + 1)
        return carry

    lax.fori_loop(2, z + 1, step, 0)

    @pl.when(jnp.logical_not(first))
    def _():
        use(0)

    def att_copy(c):
        at = slice(c * group * HD, (c + 1) * group * HD)
        return pltpu.make_async_copy(att_ref.at[:, at], att_hbm.at[:, at], out_sem.at[c])

    for h in range(heads):
        c, i = h // group, h % group
        at = slice(i * tok, (i + 1) * tok)
        total = jnp.sum(den_ref[c, at, :], axis=-1, keepdims=True)
        att_ref[:, h * HD : (h + 1) * HD] = (acc_ref[c, at, :] / total).astype(BF16)
        if i == group - 1:
            att_copy(c).start()

    ret_copy.wait()
    for c in range(kvh):
        att_copy(c).wait()
    for j in range(half):
        f_copy(j).wait_send()
        e_copy(j).wait_send()

        @pl.when(jnp.logical_not(last))
        def _():
            s_copy(j).wait_send()

    for c in range(kvh):
        p1_copy(c, 0).wait_send()
        p1_copy(c, 1).wait_send()
        p2_copy(c).wait_send()

        @pl.when(y == 0)
        def _():
            y_copy(z, c).wait_send()

        @pl.when(jnp.logical_not(last))
        def _():
            z_copy(z, c).wait_send()

    def drain(zz, carry):
        for c in range(kvh):
            y_copy(zz, c).wait_send()

            @pl.when(jnp.logical_not(last))
            def _():
                z_copy(zz, c).wait_send()

        return carry

    lax.fori_loop(0, z, drain, 0)


def hand_over(ret_in, att_in, ret_out, att_out, sem):
    copies = []
    rows = ret_in.shape[0] // 2
    for i, (src, dst) in enumerate(((ret_in, ret_out), (att_in, att_out))):
        for j in range(2):
            at = pl.ds(j * rows, rows)
            copies.append(pltpu.make_async_copy(src.at[at], dst.at[at], sem.at[i, j]))
    for copy in copies:
        copy.start()
    for copy in copies:
        copy.wait()


def body(nctx, nhg, query, key, value, gate_logit, exponent, norm_gain, kv_weight, cross_query):
    tok, width = query.shape
    heads = width // HD
    half = heads // 2
    nz = nctx // 2
    share = kv_weight.shape[1] // nhg
    kvh = share // (2 * HD)
    rows = heads // kvh * tok
    hbm = pl.BlockSpec(memory_space=pltpu.HBM)
    dma = pltpu.SemaphoreType.DMA
    results = pl.pallas_call(
        functools.partial(kernel, nz, nhg),
        out_shape=(
            jax.ShapeDtypeStruct((tok, width), BF16),
            jax.ShapeDtypeStruct((tok, width), BF16),
        ),
        in_specs=[hbm] * 8,
        out_specs=(hbm, hbm),
        scratch_shapes=[
            pltpu.VMEM((tok, width), BF16),
            pltpu.VMEM((tok, width), BF16),
            pltpu.VMEM((tok, width), BF16),
            pltpu.VMEM((tok, width), BF16),
            pltpu.VMEM((tok, width), BF16),
            pltpu.VMEM((tok, width), BF16),
            pltpu.VMEM((heads, tok), F32),
            pltpu.VMEM((1, heads), jnp.int32),
            pltpu.VMEM((heads, HD), F32),
            pltpu.VMEM((HD, tok), F32),
            pltpu.VMEM(kv_weight.shape, BF16),
            pltpu.VMEM((heads, tok, HD), F32),
            pltpu.VMEM((HD, tok), F32),
            pltpu.VMEM((-(-heads // 8) * 8, HD), F32),
            pltpu.VMEM((heads, tok, HD), F32),
            pltpu.VMEM((half, HD, HD), F32),
            pltpu.VMEM((half, HD, HD), F32),
            pltpu.VMEM((half, HD, HD), F32),
            pltpu.VMEM((-(-heads // 8) * 8, HD), F32),
            pltpu.VMEM((half, HD, HD), F32),
            pltpu.VMEM((half, HD, HD), F32),
            pltpu.VMEM((half, HD, HD), F32),
            pltpu.VMEM((half, HD, HD), F32),
            pltpu.VMEM((kvh, 2, tok, 2 * HD), F32),
            pltpu.VMEM((kvh, 2, tok, 2 * HD), F32),
            pltpu.VMEM((kvh, tok, 2 * HD), F32),
            pltpu.VMEM((kvh, tok, 2 * HD), F32),
            pltpu.VMEM((kvh, tok, 2 * HD), F32),
            pltpu.VMEM((kvh, nctx * tok, 2 * HD), BF16),
            pltpu.VMEM((kvh, rows, HD), BF16),
            pltpu.VMEM((kvh, rows, HD), F32),
            pltpu.VMEM((kvh, rows, HD), F32),
            pltpu.VMEM((kvh, rows, HD), F32),
            dma((8,)),
            dma((1 + kvh,)),
            dma((2,)),
            dma((half,)), dma((half,)), dma((half,)), dma((half,)), dma((half,)), dma((half,)),
            dma((kvh, 2)), dma((kvh, 2)), dma((kvh,)), dma((kvh,)),
            dma((nz, kvh)), dma((nz, kvh)), dma((nz, kvh)), dma((nz, kvh)),
        ],
        compiler_params=pltpu.CompilerParams(
            collective_id=0, has_side_effects=True, vmem_limit_bytes=56 * 1024 * 1024
        ),
    )(
        query, key, value, gate_logit.T, exponent.reshape(1, heads),
        norm_gain.reshape(heads, HD), kv_weight, cross_query,
    )
    return pl.pallas_call(
        hand_over,
        out_shape=(
            jax.ShapeDtypeStruct((tok, width), BF16),
            jax.ShapeDtypeStruct((tok, width), BF16),
        ),
        in_specs=[hbm, hbm],
        out_specs=(hbm, hbm),
        scratch_shapes=[dma((2, 2))],
        compiler_params=pltpu.CompilerParams(vmem_limit_bytes=56 * 1024 * 1024),
    )(*results)


def solution(mesh):
    spec = P("ctx", "hg")
    in_specs = (spec, spec, spec, spec, P("hg"), P("hg"), P("hg", None), spec)
    return jax.shard_map(
        functools.partial(body, mesh.shape["ctx"], mesh.shape["hg"]),
        mesh=mesh, in_specs=in_specs, out_specs=(spec, spec), check_vma=False,
    )
```

```python
import functools

import jax
import jax.numpy as jnp
from jax import lax
from jax.experimental import pallas as pl
from jax.experimental.pallas import tpu as pltpu
from jax.sharding import PartitionSpec as P

HD = 128
F32 = jnp.float32
BF16 = jnp.bfloat16
MESH = pl.DeviceIdType.MESH


def dot(a, b, dims=((1,), (0,))):
    return lax.dot_general(a, b, (dims, ((), ())), preferred_element_type=F32)


def carry(q, state):
    hi, lo = split(state)
    return dot(q, hi) + dot(q, lo)


def split(x):
    hi = x.astype(BF16)
    return hi, (x - hi.astype(F32)).astype(BF16)


def kernel(
    nz, nhg,
    q_hbm, k_hbm, v_hbm, gate_hbm, expo_hbm, gain_hbm, w_hbm, cq_hbm,
    ret_hbm, att_hbm,
    ret_ref, att_ref, q_ref, k_ref, v_ref, cq_ref, gate_ref, expo_ref, gain_ref, gate_pad,
    w_vm, bcol, brow, dtot_ref, local_ref,
    own_f, send_f, recv_f, recv_d, send_s, recv_s, send_e, recv_e,
    p1_send, p1_recv, p2_send, p2_recv, own_p,
    kv, cross, top_ref, den_ref, acc_ref,
    in_sem, out_sem, d_sem, fs, fr, ss, sr, es, er, p1s, p1r, p2s, p2r, zs, zr, ys, yr,
):
    tok, width = q_ref.shape
    heads = width // HD
    half = heads // 2
    share = w_vm.shape[1] // nhg
    kvh = share // (2 * HD)
    group = heads // kvh
    rows = group * tok
    scale = HD ** (-0.5)
    me = lax.axis_index("ctx")
    g = lax.axis_index("hg")
    z = me // 2
    y = me % 2
    partner = {"ctx": me + 1 - 2 * y, "hg": g}
    ahead = {"ctx": me + 2, "hg": g}
    behind = {"ctx": me - 2, "hg": g}
    g1 = g + 1 - 2 * (g % 2)
    g2 = (g + nhg // 2) % nhg
    g3 = (g1 + nhg // 2) % nhg
    near = {"ctx": me, "hg": g1}
    far = {"ctx": me, "hg": g2}
    first = z == 0
    last = z == nz - 1

    copies = [
        pltpu.make_async_copy(src, dst, in_sem.at[i])
        for i, (src, dst) in enumerate((
            (gate_hbm, gate_ref), (expo_hbm, expo_ref), (k_hbm, k_ref), (v_hbm, v_ref),
            (q_hbm, q_ref), (cq_hbm, cq_ref), (gain_hbm, gain_ref), (w_hbm, w_vm),
        ))
    ]
    for copy in copies:
        copy.start()
    gate_copy, expo_copy, k_copy, v_copy, q_copy, cq_copy, gain_copy, w_copy = copies

    barrier = pltpu.get_barrier_semaphore()
    for who in (partner, near, far):
        pl.semaphore_signal(barrier, inc=1, device_id=who, device_id_type=MESH)

    @pl.when(jnp.logical_not(first))
    def _():
        pl.semaphore_signal(barrier, inc=1, device_id=behind, device_id_type=MESH)

    @pl.when(jnp.logical_not(last))
    def _():
        pl.semaphore_signal(barrier, inc=1, device_id=ahead, device_id_type=MESH)

    def send(src, dst, s_sem, r_sem, who):
        return pltpu.make_async_remote_copy(
            src_ref=src, dst_ref=dst, send_sem=s_sem, recv_sem=r_sem,
            device_id=who, device_id_type=MESH,
        )

    def cols(h, n=HD):
        return pl.ds(pl.multiple_of(h * n, n), n)

    gate_copy.wait()
    expo_copy.wait()
    x = gate_ref[...]
    rate = jnp.exp2(-expo_ref[...].astype(F32))
    rate = jnp.concatenate([rate, jnp.zeros((1, HD - heads), F32)], axis=1)
    gate_pad[...] = jnp.zeros_like(gate_pad)
    gate_pad[:heads, :] = jnp.minimum(x, 0.0) - jnp.log1p(jnp.exp(-jnp.abs(x)))
    log_gate = jnp.transpose(gate_pad[...]) * rate
    r_id = lax.broadcasted_iota(jnp.int32, (tok, tok), 0)
    c_id = lax.broadcasted_iota(jnp.int32, (tok, tok), 1)
    lower = r_id >= c_id
    cumul = lax.dot_general(
        lower.astype(F32), log_gate, (((1,), (0,)), ((), ())),
        precision=lax.Precision.HIGHEST, preferred_element_type=F32,
    )
    brow[...] = jnp.transpose(cumul)
    for h in range(heads):
        bcol[h] = jnp.broadcast_to(cumul[:, h : h + 1], (tok, HD))

    pad = dtot_ref.shape[0]
    dtot_ref[...] = jnp.exp(jnp.broadcast_to(brow[:pad, tok - 1 : tok], (pad, HD)))

    def fresh(h):
        total = bcol[h, tok - 1 : tok, :]
        keys = k_ref[:, cols(h)].astype(F32) * (jnp.exp(total - bcol[h]) * scale)
        hi, lo = split(keys)
        vals = v_ref[:, cols(h)]
        dims = ((0,), (0,))
        return dot(hi, vals, dims) + dot(lo, vals, dims)

    pl.semaphore_wait(barrier, 3 + jnp.where(first, 0, 1) + jnp.where(last, 0, 1))

    k_copy.wait()
    v_copy.wait()
    d_copy = send(dtot_ref, recv_d, d_sem.at[0], d_sem.at[1], partner)
    d_copy.start()
    for j in range(half):
        send_f[j] = fresh((1 - y) * half + j)
        send(send_f.at[j], recv_f.at[j], fs.at[j], fr.at[j], partner).start()
    for j in range(half):
        own_f[j] = fresh(y * half + j)

    def pair(j):
        mine, his = own_f[j], recv_f[j]
        row = pl.ds(y * half + j, 1)
        dm, dh = dtot_ref[row, :], recv_d[row, :]
        even = y == 0
        f0, f1 = jnp.where(even, mine, his), jnp.where(even, his, mine)
        d0, d1 = jnp.where(even, dm, dh), jnp.where(even, dh, dm)
        return f0, f1, d0, d1

    def f_copy(j):
        return send(send_f.at[j], recv_f.at[j], fs.at[j], fr.at[j], partner)

    def s_copy(j):
        return send(send_s.at[j], recv_s.at[j], ss.at[j], sr.at[j], ahead)

    def e_copy(j):
        return send(send_e.at[j], recv_e.at[j], es.at[j], er.at[j], partner)

    @pl.when(first)
    def _():
        recv_s[...] = jnp.zeros_like(recv_s)

    d_copy.wait()
    for j in range(half):
        f_copy(j).wait_recv()
        f0, f1, d0, d1 = pair(j)
        send_s[j] = d1 * f0 + f1

        @pl.when(first)
        def _():
            s_copy(j).start()

    q_copy.wait()
    for h in range(heads):
        diff = jnp.minimum(bcol[h] - brow[h : h + 1, :], 0.0)
        decay = jnp.where(lower, jnp.exp(diff), 0.0)
        at = slice(h * HD, (h + 1) * HD)
        score = dot(q_ref[:, at], k_ref[:, at], ((1,), (1,)))
        weight = (score * decay * scale).astype(BF16)
        local_ref[h] = dot(weight, v_ref[:, at])

    cq_copy.wait()
    gain_copy.wait()
    for h in range(heads):
        c, i = h // group, h % group
        cross[c, i * tok : (i + 1) * tok, :] = cq_ref[:, h * HD : (h + 1) * HD]
    top_ref[...] = jnp.full_like(top_ref, -1e30)
    den_ref[...] = jnp.zeros_like(den_ref)
    acc_ref[...] = jnp.zeros_like(acc_ref)

    def finish(h, state):
        out = local_ref[h] + carry(q_ref[:, cols(h)], state) * jnp.exp(bcol[h])
        mean = jnp.mean(out, axis=-1, keepdims=True)
        out = out - mean
        var = jnp.mean(out * out, axis=-1, keepdims=True)
        out = out / jnp.sqrt(var + 1e-06) * gain_ref[pl.ds(h, 1), :]
        ret_ref[:, cols(h)] = out.astype(BF16)

    lag = min(2, half)
    for j in range(half):
        @pl.when(jnp.logical_not(first))
        def _():
            s_copy(j).wait_recv()
            _, _, d0, d1 = pair(j)
            send_s[j] = (d0 * d1) * recv_s[j] + send_s[j]

            @pl.when(jnp.logical_not(last))
            def _():
                s_copy(j).start()

        f0, _, d0, _ = pair(j)
        s = recv_s[j]
        e1 = d0 * s + f0
        send_e[j] = jnp.where(y == 0, e1, s)
        e_copy(j).start()
        finish(y * half + j, jnp.where(y == 0, s, e1))
        if j >= lag:
            e_copy(j - lag).wait_recv()
            finish((1 - y) * half + j - lag, recv_e[j - lag])
    for j in range(half - lag, half):
        e_copy(j).wait_recv()
    for j in range(half - lag, half):
        finish((1 - y) * half + j, recv_e[j])

    ret_copy = pltpu.make_async_copy(ret_ref, ret_hbm, out_sem.at[kvh])
    ret_copy.start()
    w_copy.wait()
    wide = 2 * HD

    def p1_copy(c, b):
        return send(p1_send.at[c, b], p1_recv.at[c, b], p1s.at[c, b], p1r.at[c, b], near)

    def p2_copy(c):
        return send(p2_send.at[c], p2_recv.at[c], p2s.at[c], p2r.at[c], far)

    def part(dest, c):
        return dot(ret_ref[...], w_vm[:, cols(dest * kvh + c, wide)])

    for c in range(kvh):
        p1_send[c, 0] = part(g3, c)
        p1_copy(c, 0).start()
    for c in range(kvh):
        p2_send[c] = part(g2, c)
        p1_copy(c, 0).wait_recv()
        p2_send[c] = p2_send[c] + p1_recv[c, 0]
        p2_copy(c).start()
    for c in range(kvh):
        p1_send[c, 1] = part(g1, c)
        p1_copy(c, 1).start()
    for c in range(kvh):
        own_p[c] = part(g, c)
    for c in range(kvh):
        p1_copy(c, 1).wait_recv()
        own_p[c] = own_p[c] + p1_recv[c, 1]

    def spot(block, c):
        return kv.at[c, pl.ds(pl.multiple_of(block * tok, tok), tok), :]

    def z_copy(zz, c):
        at = spot(2 * zz + y, c)
        return send(at, at, zs.at[zz, c], zr.at[zz, c], ahead)

    def y_copy(zz, c):
        at = spot(2 * zz + y, c)
        return send(at, at, ys.at[zz, c], yr.at[zz, c], partner)

    def y_arrived(zz, c):
        at = spot(2 * zz + 1 - y, c)
        return send(at, at, ys.at[zz, c], yr.at[zz, c], partner)

    def attend(zz, c, masked):
        both = kv[c, pl.ds(pl.multiple_of(zz * 2 * tok, 2 * tok), 2 * tok), :]
        keys, vals = both[:, :HD], both[:, HD:]
        score = dot(cross[c], keys, ((1,), (1,))) * scale
        if masked:
            q_pos = y * tok + lax.broadcasted_iota(jnp.int32, (tok, 2 * tok), 0)
            keep = lax.broadcasted_iota(jnp.int32, (tok, 2 * tok), 1) <= q_pos
            keep = jnp.concatenate([jnp.where(keep, 1.0, 0.0)] * group, axis=0) > 0.5
            score = jnp.where(keep, score, -1e30)
        old = top_ref[c]
        new = jnp.maximum(old, jnp.max(score, axis=-1, keepdims=True))
        factor = jnp.exp(old - new)
        top_ref[c] = new
        expo = jnp.exp(score - jnp.concatenate([new, new], axis=1))
        if masked:
            expo = jnp.where(keep, expo, 0.0)
        den_ref[c] = den_ref[c] * factor + (expo[:, :HD] + expo[:, HD:])
        acc_ref[c] = acc_ref[c] * factor + dot(expo.astype(BF16), vals)

    for c in range(kvh):
        p2_copy(c).wait_recv()
        spot(me, c)[...] = (own_p[c] + p2_recv[c]).astype(BF16)

        @pl.when(y == 0)
        def _():
            y_copy(z, c).start()
            spot(me + 1, c)[...] = jnp.zeros((tok, wide), BF16)

        @pl.when(jnp.logical_not(last))
        def _():
            z_copy(z, c).start()

    def relay(zz):
        for c in range(kvh):
            z_copy(zz, c).wait_recv()

            @pl.when(jnp.logical_not(last))
            def _():
                z_copy(zz, c).start()

            y_copy(zz, c).start()

    def use(zz):
        for c in range(kvh):
            y_arrived(zz, c).wait_recv()
            attend(zz, c, False)

    @pl.when(jnp.logical_not(first))
    def _():
        relay(z - 1)

    for c in range(kvh):
        @pl.when(y == 1)
        def _():
            y_arrived(z, c).wait_recv()

        attend(z, c, True)

    def step(n, carry):
        relay(z - n)
        use(z - n + 1)
        return carry

    lax.fori_loop(2, z + 1, step, 0)

    @pl.when(jnp.logical_not(first))
    def _():
        use(0)

    def att_copy(c):
        at = slice(c * group * HD, (c + 1) * group * HD)
        return pltpu.make_async_copy(att_ref.at[:, at], att_hbm.at[:, at], out_sem.at[c])

    for h in range(heads):
        c, i = h // group, h % group
        at = slice(i * tok, (i + 1) * tok)
        total = jnp.sum(den_ref[c, at, :], axis=-1, keepdims=True)
        att_ref[:, h * HD : (h + 1) * HD] = (acc_ref[c, at, :] / total).astype(BF16)
        if i == group - 1:
            att_copy(c).start()

    ret_copy.wait()
    for c in range(kvh):
        att_copy(c).wait()
    for j in range(half):
        f_copy(j).wait_send()
        e_copy(j).wait_send()

        @pl.when(jnp.logical_not(last))
        def _():
            s_copy(j).wait_send()

    for c in range(kvh):
        p1_copy(c, 0).wait_send()
        p1_copy(c, 1).wait_send()
        p2_copy(c).wait_send()

        @pl.when(y == 0)
        def _():
            y_copy(z, c).wait_send()

        @pl.when(jnp.logical_not(last))
        def _():
            z_copy(z, c).wait_send()

    def drain(zz, carry):
        for c in range(kvh):
            y_copy(zz, c).wait_send()

            @pl.when(jnp.logical_not(last))
            def _():
                z_copy(zz, c).wait_send()

        return carry

    lax.fori_loop(0, z, drain, 0)


def hand_over(ret_in, att_in, ret_out, att_out, held, in_sem, out_sem):
    moves = []
    rows = ret_in.shape[0] // 2
    for i, (src, dst) in enumerate(((ret_in, ret_out), (att_in, att_out))):
        for j in range(2):
            at = pl.ds(j * rows, rows)
            spot = held.at[i, at]
            moves.append((
                pltpu.make_async_copy(src.at[at], spot, in_sem.at[i, j]),
                pltpu.make_async_copy(spot, dst.at[at], out_sem.at[i, j]),
            ))
    for load, _ in moves:
        load.start()
    for load, store in moves:
        load.wait()
        store.start()
    for _, store in moves:
        store.wait()


def body(nctx, nhg, query, key, value, gate_logit, exponent, norm_gain, kv_weight, cross_query):
    tok, width = query.shape
    heads = width // HD
    half = heads // 2
    nz = nctx // 2
    share = kv_weight.shape[1] // nhg
    kvh = share // (2 * HD)
    rows = heads // kvh * tok
    hbm = pl.BlockSpec(memory_space=pltpu.HBM)
    dma = pltpu.SemaphoreType.DMA
    results = pl.pallas_call(
        functools.partial(kernel, nz, nhg),
        out_shape=(
            jax.ShapeDtypeStruct((tok, width), BF16),
            jax.ShapeDtypeStruct((tok, width), BF16),
        ),
        in_specs=[hbm] * 8,
        out_specs=(hbm, hbm),
        scratch_shapes=[
            pltpu.VMEM((tok, width), BF16),
            pltpu.VMEM((tok, width), BF16),
            pltpu.VMEM((tok, width), BF16),
            pltpu.VMEM((tok, width), BF16),
            pltpu.VMEM((tok, width), BF16),
            pltpu.VMEM((tok, width), BF16),
            pltpu.VMEM((heads, tok), F32),
            pltpu.VMEM((1, heads), jnp.int32),
            pltpu.VMEM((heads, HD), F32),
            pltpu.VMEM((HD, tok), F32),
            pltpu.VMEM(kv_weight.shape, BF16),
            pltpu.VMEM((heads, tok, HD), F32),
            pltpu.VMEM((HD, tok), F32),
            pltpu.VMEM((-(-heads // 8) * 8, HD), F32),
            pltpu.VMEM((heads, tok, HD), F32),
            pltpu.VMEM((half, HD, HD), F32),
            pltpu.VMEM((half, HD, HD), F32),
            pltpu.VMEM((half, HD, HD), F32),
            pltpu.VMEM((-(-heads // 8) * 8, HD), F32),
            pltpu.VMEM((half, HD, HD), F32),
            pltpu.VMEM((half, HD, HD), F32),
            pltpu.VMEM((half, HD, HD), F32),
            pltpu.VMEM((half, HD, HD), F32),
            pltpu.VMEM((kvh, 2, tok, 2 * HD), F32),
            pltpu.VMEM((kvh, 2, tok, 2 * HD), F32),
            pltpu.VMEM((kvh, tok, 2 * HD), F32),
            pltpu.VMEM((kvh, tok, 2 * HD), F32),
            pltpu.VMEM((kvh, tok, 2 * HD), F32),
            pltpu.VMEM((kvh, nctx * tok, 2 * HD), BF16),
            pltpu.VMEM((kvh, rows, HD), BF16),
            pltpu.VMEM((kvh, rows, HD), F32),
            pltpu.VMEM((kvh, rows, HD), F32),
            pltpu.VMEM((kvh, rows, HD), F32),
            dma((8,)),
            dma((1 + kvh,)),
            dma((2,)),
            dma((half,)), dma((half,)), dma((half,)), dma((half,)), dma((half,)), dma((half,)),
            dma((kvh, 2)), dma((kvh, 2)), dma((kvh,)), dma((kvh,)),
            dma((nz, kvh)), dma((nz, kvh)), dma((nz, kvh)), dma((nz, kvh)),
        ],
        compiler_params=pltpu.CompilerParams(
            collective_id=0, has_side_effects=True, vmem_limit_bytes=56 * 1024 * 1024
        ),
    )(
        query, key, value, gate_logit.T, exponent.reshape(1, heads),
        norm_gain.reshape(heads, HD), kv_weight, cross_query,
    )
    return pl.pallas_call(
        hand_over,
        out_shape=(
            jax.ShapeDtypeStruct((tok, width), BF16),
            jax.ShapeDtypeStruct((tok, width), BF16),
        ),
        in_specs=[hbm, hbm],
        out_specs=(hbm, hbm),
        scratch_shapes=[pltpu.VMEM((2, tok, width), BF16), dma((2, 2)), dma((2, 2))],
        compiler_params=pltpu.CompilerParams(vmem_limit_bytes=56 * 1024 * 1024),
    )(*results)


def solution(mesh):
    spec = P("ctx", "hg")
    in_specs = (spec, spec, spec, spec, P("hg"), P("hg"), P("hg", None), spec)
    return jax.shard_map(
        functools.partial(body, mesh.shape["ctx"], mesh.shape["hg"]),
        mesh=mesh, in_specs=in_specs, out_specs=(spec, spec), check_vma=False,
    )
```
